32 devices in a mesh: node: 8 (over y, x, core), local: 4 (over z).
Axes of the slice: x: 2, y: 2, z: 4, core: 2. Of those that a mesh axis runs over, the one named last changes fastest.
Arguments:
- tokens_x: bfloat16 [4096, 2048], P(('node', 'local')), may hold values from -6 to 6
- grad_out: bfloat16 [4096, 2048], P(('node', 'local')), may hold values from -6 to 6
- expert_ids: int32 [4096, 8], P(('node', 'local')), may hold values from 0 to 31, all different within a row; in each aligned block of 128 rows (0 to 127, 128 to 255, ...) at most 33 rows name the same one
- probs: bfloat16 [4096, 8], P(('node', 'local')), may hold values from 0.049804688 to 0.34960938
- w_gate: bfloat16 [32, 2048, 768], P(('node', 'local')), may hold values from -0.125 to 0.125
- w_up: bfloat16 [32, 2048, 768], P(('node', 'local')), may hold values from -0.125 to 0.125
- w_down: bfloat16 [32, 768, 2048], P(('node', 'local')), may hold values from -0.21875 to 0.21875
Outputs:
- grad_x: bfloat16 [4096, 2048], P(('node', 'local'))
- grad_probs: bfloat16 [4096, 8], P(('node', 'local'))
- grad_gate: bfloat16 [32, 2048, 768], P(('node', 'local'))
- grad_up: bfloat16 [32, 2048, 768], P(('node', 'local'))
- grad_down: bfloat16 [32, 768, 2048], P(('node', 'local'))
The draws below stay inside these ranges and needn't reach their ends.
Inputs may be any that keep to these rules, and one draw needn't show every extreme that they name: `expert_ids`: each row names 8 different experts; among the 128 tokens of one device no expert is named more than 33 times, a bound that some block reaches.
All inputs are finite; a program needn't handle non-finite values.
Results may differ from the reference program's by a relative error of at most 0.0065.
Values may be sent and summed in bfloat16 or wider, within the bound.
No kernel may reach another device: no remote copies, remote signals or barrier semaphores. Data moves between devices by JAX's collectives and lax.ppermute only.
A program may use at most 128 MiB of HBM per device.

```python
import math
import jax
import jax.numpy as jnp
import numpy as np
from jax import lax

D = 2048
FF = 768
TOP = 8
TOK_DEV = 128
EXPERTS = 32
TOKENS = 4096
CAP = 33
N_NODE = 8
N_LOCAL = 4


def shard_levels(key, extent, cuts, least, top_value):
    gain, own = 1.0, jax.random.fold_in(key, 6)
    for position, shards_of in cuts:
        steps = jnp.exp(jax.random.uniform(jax.random.fold_in(own, position), (shards_of,), jnp.float32, least / len(cuts), top_value / len(cuts)))
        gain = gain * jnp.repeat(steps, extent[position] // shards_of).reshape([-1 if axis == position else 1 for axis in range(len(extent))])
    return gain


def routed_block(rng, own, number, rows, number_of, top, reach, skew):
    order = jax.random.permutation(rng, number_of)
    packed, ordinary = portions_of(number_of, rows * top, reach, skew, True), portions_of(number_of, rows * top, reach, skew, False)
    places = jnp.arange(number_of)

    def named(lengths, turn):
        used = int((lengths > 0).sum())
        fixed = max(1, used // 4)
        passed = fixed + (places - fixed + turn * (used - fixed)) % max(1, number_of - fixed)
        return jnp.zeros((number_of,), jnp.int32).at[order[jnp.where(places < fixed, places, passed)]].set(jnp.asarray(lengths, jnp.int32))

    lengths = jnp.where(number % 4 == 0, named(packed, number // 4), named(ordinary, number - number // 4 - 1))
    mixed = jax.random.permutation(jax.random.fold_in(own, 3), number_of)
    giver, receiver = mixed[0:number_of // 2 * 2:2], mixed[1:number_of // 2 * 2:2]
    room = jnp.minimum(lengths[giver] - 1, reach - lengths[receiver]) // 2
    room = jnp.where((giver == order[0]) | (receiver == order[0]) | (lengths[receiver] == 0), 0, jnp.maximum(room, 0))
    passed = jax.random.randint(jax.random.fold_in(own, 4), (number_of // 2,), 0, 1 << 20) % (room + 1)
    lengths = lengths.at[giver].add(-passed).at[receiver].add(passed)
    members = jnp.searchsorted(jnp.cumsum(lengths), jnp.arange(rows * top), side="right").astype(jnp.int32)
    table = members.reshape(top, rows).T
    table = table[jax.random.permutation(jax.random.fold_in(own, 1), rows)]
    turn = jax.random.randint(jax.random.fold_in(own, 2), (rows, 1), 0, top)
    return jnp.take_along_axis(table, (jnp.arange(top)[None, :] + turn) % top, axis=1)


def portions_of(amount, total, most, skew, full):
    portions = [(1 << 20) // math.isqrt(rank ** skew) + 1 for rank in range(1, amount + 1)]
    largest = most if full else min(most, max(-(-total // amount), total * portions[0] // sum(portions)))
    least = 1 if total - largest >= amount - 1 else 0
    counts, rest = [largest] + [least] * (amount - 1), total - largest - least * (amount - 1)
    while rest > 0:
        free = [i for i in range(1, amount) if counts[i] < largest] or [i for i in range(1, amount) if counts[i] < most]
        mass, budget = sum([portions[i] for i in free]), rest
        for i in free:
            more = min(most - counts[i], max(1, budget * portions[i] // mass), rest)
            counts[i] = counts[i] + more
            rest = rest - more
    return np.array(counts)


def bell_draw(rng, dims, deviation, reach, pieces=(), kind=jnp.bfloat16):
    array = deviation * jax.random.normal(rng, dims, jnp.float32)
    if pieces:
        array = array * shard_levels(rng, dims, pieces, -0.22, 0.18)
    return jnp.clip(array, -reach, reach).astype(kind)


def setup_inputs(seed: int = 0) -> dict:
    seeds = jax.random.split(jax.random.key(seed), 8)
    tokens_x = bell_draw(seeds[0], (TOKENS, D), 1.0, 6.0, ((0, 32),))
    grad_out = bell_draw(seeds[1], (TOKENS, D), 1.0, 6.0, ((0, 32),))
    expert_ids_keys = jax.random.split(jax.random.fold_in(seeds[2], 1), TOKENS // TOK_DEV)
    expert_ids_turns = jax.random.permutation(jax.random.fold_in(seeds[2], 3), TOKENS // TOK_DEV)
    expert_ids = jax.vmap(lambda own, number: routed_block(jax.random.fold_in(seeds[2], 2), own, number, TOK_DEV, EXPERTS, TOP, CAP, 2))(expert_ids_keys, expert_ids_turns).reshape((TOKENS, TOP))
    probs = jnp.clip(0.049804688 + 0.2998047 * jax.random.uniform(seeds[3], (TOKENS, TOP), jnp.float32) ** shard_levels(seeds[3], (TOKENS, TOP), ((0, 32),), -0.2, 0.2), 0.049804688, 0.34960938).astype(jnp.bfloat16)
    w_gate = bell_draw(seeds[4], (EXPERTS, D, FF), D ** -0.5, 0.125, ((0, 32),))
    w_up = bell_draw(seeds[5], (EXPERTS, D, FF), D ** -0.5, 0.125, ((0, 32),))
    w_down = bell_draw(seeds[6], (EXPERTS, FF, D), FF ** -0.5, 0.21875, ((0, 32),))
    return {"tokens_x": tokens_x, "grad_out": grad_out, "expert_ids": expert_ids, "probs": probs, "w_gate": w_gate, "w_up": w_up, "w_down": w_down}


def expert_backward(rows_x, rows_dy, rows_p, gate_e, up_e, down_e):
    gate_pre = jnp.dot(rows_x, gate_e, preferred_element_type=jnp.float32)
    up_pre = jnp.dot(rows_x, up_e, preferred_element_type=jnp.float32)
    sigmoid_g = jax.nn.sigmoid(gate_pre)
    activated = gate_pre * sigmoid_g
    hidden_f = activated * up_pre
    hidden_grad = lax.dot_general(rows_dy, down_e, (((1,), (1,)), ((), ())), preferred_element_type=jnp.float32)
    prob_grad = jnp.sum(hidden_grad * hidden_f, axis=1).astype(jnp.bfloat16)
    weight_col = rows_p.astype(jnp.float32)[:, None]
    scaled_grad = hidden_grad * weight_col
    weighted_hidden = (hidden_f * weight_col).astype(jnp.bfloat16)
    up_rows = (scaled_grad * activated).astype(jnp.bfloat16)
    gate_rows = (scaled_grad * up_pre * sigmoid_g * (1.0 + gate_pre * (1.0 - sigmoid_g))).astype(jnp.bfloat16)
    input_grad = lax.dot_general(gate_rows, gate_e, (((1,), (1,)), ((), ())), preferred_element_type=jnp.float32)
    input_grad = input_grad + lax.dot_general(up_rows, up_e, (((1,), (1,)), ((), ())), preferred_element_type=jnp.float32)
    input_grad = input_grad.astype(jnp.bfloat16)
    gate_wgrad = lax.dot_general(rows_x, gate_rows, (((0,), (0,)), ((), ())), preferred_element_type=jnp.float32).astype(jnp.bfloat16)
    up_wgrad = lax.dot_general(rows_x, up_rows, (((0,), (0,)), ((), ())), preferred_element_type=jnp.float32).astype(jnp.bfloat16)
    down_wgrad = lax.dot_general(weighted_hidden, rows_dy, (((0,), (0,)), ((), ())), preferred_element_type=jnp.float32).astype(jnp.bfloat16)
    return input_grad, prob_grad, gate_wgrad, up_wgrad, down_wgrad


def reference(tokens_x, grad_out, expert_ids, probs, w_gate, w_up, w_down):
    devices = N_NODE * N_LOCAL
    per_device = TOK_DEV * TOP
    routed = expert_ids.reshape(devices, per_device).astype(jnp.int32)
    expert_row = jnp.arange(EXPERTS, dtype=jnp.int32)
    one_hot = (routed[:, :, None] == expert_row[None, None, :]).astype(jnp.int32)
    earlier = jnp.cumsum(one_hot, axis=1) - 1
    slot_index = jnp.sum(earlier * one_hot, axis=2).astype(jnp.int32)
    device_rows = jnp.broadcast_to(jnp.arange(devices, dtype=jnp.int32)[:, None], routed.shape)
    global_rows = device_rows * per_device + jnp.arange(per_device, dtype=jnp.int32)[None, :]
    table = jnp.full((devices, EXPERTS, CAP), TOKENS * TOP, jnp.int32)
    table = table.at[device_rows, routed, slot_index].set(global_rows)
    padded_x = jnp.concatenate([tokens_x, jnp.zeros((1, D), jnp.bfloat16)], axis=0)
    padded_dy = jnp.concatenate([grad_out, jnp.zeros((1, D), jnp.bfloat16)], axis=0)
    padded_p = jnp.concatenate([probs.reshape(-1), jnp.zeros((1,), jnp.bfloat16)], axis=0)

    def one_expert(carry, expert):
        input_acc, prob_acc = carry
        rows = table[:, expert, :].reshape(-1)
        token_rows = rows // TOP
        result = expert_backward(padded_x[token_rows], padded_dy[token_rows], padded_p[rows],
                                 w_gate[expert], w_up[expert], w_down[expert])
        input_acc = input_acc.at[token_rows].add(result[0].astype(jnp.float32))
        prob_acc = prob_acc.at[rows].add(result[1].astype(jnp.float32))
        return (input_acc, prob_acc), (result[2], result[3], result[4])

    start = (jnp.zeros((TOKENS + 1, D), jnp.float32), jnp.zeros((TOKENS * TOP + 1,), jnp.float32))
    (input_acc, prob_acc), grads = lax.scan(one_expert, start, jnp.arange(EXPERTS, dtype=jnp.int32))
    grad_x = input_acc[:TOKENS].astype(jnp.bfloat16)
    grad_probs = prob_acc[:TOKENS * TOP].reshape(TOKENS, TOP).astype(jnp.bfloat16)
    return grad_x, grad_probs, grads[0], grads[1], grads[2]
```

```python
import functools

import jax
import jax.numpy as jnp
from jax import lax
from jax.experimental import pallas as pl
from jax.experimental.pallas import tpu as pltpu
from jax.sharding import PartitionSpec as P

F32 = jnp.float32
BF16 = jnp.bfloat16
NT = (((1,), (1,)), ((), ()))
TN = (((0,), (0,)), ((), ()))
LANES = 128
EXTRA = 16
TAIL = 8


def pad_to(value, unit):
    return -(-value // unit) * unit


class Rows:
    def __init__(self, cap):
        self.slots = 2 * cap
        self.base = self.slots // 16 * 16
        self.shift = self.slots - self.base
        self.group = pad_to(self.slots + self.shift + 1, 8)
        self.prob = 2 * self.slots
        self.message = max(pad_to(self.prob + 1, 8), self.base + self.group)


def iota(shape, dim):
    return lax.broadcasted_iota(jnp.int32, shape, dim)


def eye(rows):
    return jnp.where(iota((rows, LANES), 0) == iota((rows, LANES), 1), 1.0, 0.0).astype(BF16)


def ranks(info_ref, w_refs, first, targets):
    place = iota((EXTRA, LANES), 0) == info_ref[0]
    lines = []
    for j in range(targets):
        lane = pl.multiple_of(info_ref[1 + j] * LANES, LANES)
        parts = []
        for w in w_refs:
            part = w[first : first + EXTRA, pl.ds(lane, LANES)].astype(F32)
            parts.append(jnp.sum(jnp.where(place, part, 0.0), axis=0, keepdims=True))
        lines.append(jnp.concatenate(parts, axis=1))
    tokens = lines[0].shape[1]
    lines.append(jnp.zeros((pad_to(targets, 8) - targets, tokens), F32))
    probs = jnp.concatenate([line for line in lines if line.shape[0]], axis=0)
    named = probs != 0.0
    upto = jnp.where(iota((tokens, tokens), 0) <= iota((tokens, tokens), 1), 1.0, 0.0).astype(BF16)
    count = jnp.dot(jnp.where(named, 1.0, 0.0).astype(BF16), upto, preferred_element_type=F32)
    return probs, jnp.where(named, count, -999.0)


def pick(rank, j, rows, start=0):
    slot = (iota((rows, rank.shape[1]), 0) + (1 - start)).astype(F32)
    return jnp.where(slot == rank[j : j + 1, :], 1.0, 0.0).astype(BF16)


def pack_kernel(nodes, locals_, x_ref, dy_ref, ids_ref, probs_ref, out_ref):
    tokens, width = x_ref.shape
    out_ref[:tokens, :] = x_ref[...]
    out_ref[tokens : 2 * tokens, :] = dy_ref[...]
    place = iota((EXTRA, tokens), 0)
    for n in range(width // tokens):
        line = jnp.zeros((EXTRA, tokens), F32)
        if n < nodes:
            for k in range(ids_ref.shape[0]):
                hit = (place < locals_) & (ids_ref[k : k + 1, :] == place + n * locals_)
                line = line + jnp.where(hit, probs_ref[k : k + 1, :], 0.0)
        out_ref[2 * tokens :, n * tokens : (n + 1) * tokens] = line.astype(BF16)


def dispatch_kernel(at, targets, info_ref, mine_ref, sibling_ref, *outs):
    tokens = (mine_ref.shape[0] - EXTRA) // 2
    width = mine_ref.shape[1]
    blocks = (mine_ref, sibling_ref)
    probs, rank = ranks(info_ref, blocks, 2 * tokens, targets)
    picks, lines = [], []
    for j in range(targets):
        x = pick(rank, j, at.message)
        dy = pick(rank, j, at.message, at.slots)
        picks.append(
            jnp.concatenate([x[:, :tokens], dy[:, :tokens], x[:, tokens:], dy[:, tokens:]], axis=1)
        )
        lines.append(
            lax.dot_general(
                probs.astype(BF16), pick(rank, j, LANES), NT, preferred_element_type=F32
            )[j : j + 1, :]
        )
    picks = jnp.concatenate(picks, axis=0)
    step = next(s for s in (512, 256, 128) if width % s == 0)
    for start in range(0, width, step):
        rows = jnp.concatenate([b[: 2 * tokens, start : start + step] for b in blocks], axis=0)
        out = jnp.dot(picks, rows, preferred_element_type=F32)
        for j in range(targets):
            part = out[j * at.message : (j + 1) * at.message]
            if start == 0:
                line = jnp.concatenate([lines[j], jnp.zeros((1, step - LANES), F32)], axis=1)
                part = jnp.where(iota(part.shape, 0) == at.prob, line, part)
            outs[j][:, start : start + step] = part.astype(BF16)


def combine_kernel(at, targets, info_ref, mine_ref, sibling_ref, *refs):
    rets_ref, keep_ref, send_ref = refs
    chips = [info_ref[1 + j] // 2 for j in range(targets)]
    tokens = keep_ref.shape[0] - TAIL
    width = keep_ref.shape[1]
    _, rank = ranks(info_ref, (mine_ref, sibling_ref), 0, targets)
    picks = [pick(rank, j, at.group) for j in range(targets)]
    step = next(s for s in (512, 256, 128) if width % s == 0)
    for start in range(0, width, step):
        total = None
        for j in range(targets):
            part = lax.dot_general(
                picks[j], rets_ref[chips[j], :, start : start + step], TN, preferred_element_type=F32
            )
            total = part if total is None else total + part
        keep_ref[:tokens, start : start + step] = total[:tokens].astype(BF16)
        send_ref[:tokens, start : start + step] = total[tokens:].astype(BF16)
    row = iota((TAIL, LANES), 0)
    for n in range(width // LANES):
        keep = send = jnp.zeros((TAIL, LANES), F32)
        if n < targets:
            tail = rets_ref[chips[n], at.group - 8 :, :LANES]
            line = jnp.dot(tail, pick(rank, n, LANES), preferred_element_type=F32)[7:8]
            keep = jnp.where(row == 0, line[:, :tokens], keep)
            send = jnp.where(row == 1, line[:, tokens:], send)
        keep_ref[tokens:, n * LANES : (n + 1) * LANES] = keep.astype(BF16)
        send_ref[tokens:, n * LANES : (n + 1) * LANES] = send.astype(BF16)


def expert_kernel(at, sources, aliased, info_ref, *refs):
    msgs, refs = refs[:sources], refs[sources:]
    gate_ref, up_ref, down_t_ref, gate_t_ref, up_t_ref = refs[:5]
    refs = refs[5 + aliased :]
    ret_ref, x_all, dy_all, hp_ref, du_ref, dg_ref, p_ref, dx_ref, pg_ref, moved_ref = refs
    step = pl.program_id(0)
    rows, tile = hp_ref.shape
    group, shift = at.group, at.shift

    @pl.when(step == 0)
    def _():
        x_all[...] = jnp.concatenate([m[:group, :] for m in msgs], axis=0)
        dy_all[...] = jnp.concatenate([m[at.base : at.base + group, :] for m in msgs], axis=0)
        first = at.prob // 8 * 8
        for i, m in enumerate(msgs):
            p = lax.dot_general(
                eye(group), m[first : first + 8, :LANES], NT, preferred_element_type=F32
            )
            line = at.prob - first
            p_ref[i * group : (i + 1) * group, :] = p[:, line : line + 1] + jnp.zeros(
                (group, LANES), F32
            )

    x, dy = x_all[...], dy_all[...]
    p = p_ref[:, :1]
    g = jnp.dot(x, gate_ref[0], preferred_element_type=F32)
    u = jnp.dot(x, up_ref[0], preferred_element_type=F32)
    moved_ref[:rows, :] = jnp.dot(dy, down_t_ref[...], preferred_element_type=F32)
    moved_ref[rows:, :] = jnp.zeros((8, tile), F32)
    dh = moved_ref[shift : shift + rows, :]
    s = jax.nn.sigmoid(g)
    a = g * s
    h = a * u
    sd = dh * p
    pg = jnp.sum(dh * h, axis=1, keepdims=True)
    du = (sd * a).astype(BF16)
    dg = (sd * u * s * (1.0 + g * (1.0 - s))).astype(BF16)
    du_ref[...] = du
    dg_ref[...] = dg
    moved_ref[:8, :] = jnp.zeros((8, tile), F32)
    moved_ref[shift : shift + rows, :] = h * p
    hp_ref[...] = moved_ref[:rows, :].astype(BF16)
    dx = jnp.dot(dg, gate_t_ref[...], preferred_element_type=F32)
    dx = dx + jnp.dot(du, up_t_ref[...], preferred_element_type=F32)

    @pl.when(step == 0)
    def _():
        dx_ref[...] = dx
        pg_ref[...] = pg + jnp.zeros_like(pg_ref)

    @pl.when(step > 0)
    def _():
        dx_ref[...] += dx
        pg_ref[...] += pg

    @pl.when(step == pl.num_programs(0) - 1)
    def _():
        last = iota((8, LANES), 0) == 7
        for i in range(sources):
            chip = info_ref[1 + i] // 2
            part = slice(i * group, (i + 1) * group)
            line = lax.dot_general(
                pg_ref[part, :].astype(BF16), eye(group), TN, preferred_element_type=F32
            )[:1]
            ret_ref[chip] = dx_ref[part, :].astype(BF16)
            tail = jnp.where(last, line, dx_ref[(i + 1) * group - 8 : (i + 1) * group, :LANES])
            ret_ref[chip, group - 8 :, :LANES] = tail.astype(BF16)


def whole(shape):
    return pl.BlockSpec(shape, lambda *_: (0,) * len(shape), pipeline_mode=pl.Buffered(1))


def params(mib):
    return pltpu.CompilerParams(vmem_limit_bytes=mib * 1024 * 1024)


COST = pl.CostEstimate(flops=1024, bytes_accessed=1024, transcendentals=0)


SMEM = pl.BlockSpec(memory_space=pltpu.SMEM)


def call(kernel, info, operands, out_shape, in_specs=None):
    return pl.pallas_call(
        kernel,
        grid=(1,),
        in_specs=([SMEM] if info is not None else [])
        + (in_specs or [whole(a.shape) for a in operands]),
        out_specs=[whole(s.shape) for s in out_shape],
        out_shape=out_shape,
        compiler_params=params(20),
        cost_estimate=COST,
    )(*([info] if info is not None else []), *operands)


def pack(x, dy, ids_t, probs_t, nodes, locals_):
    tokens, width = x.shape
    shape = jax.ShapeDtypeStruct((2 * tokens + EXTRA, width), BF16)
    kernel = functools.partial(pack_kernel, nodes, locals_)
    return call(kernel, None, [x, dy, ids_t, probs_t], [shape])[0]


def dispatch(at, targets, info, mine, sibling):
    height, width = mine.shape
    shapes = [jax.ShapeDtypeStruct((at.message, width), BF16)] * targets
    kernel = functools.partial(dispatch_kernel, at, targets)
    return call(kernel, info, [mine, sibling], shapes)


def combine(at, info, mine, sibling, rets):
    height, width = mine.shape
    tokens = (height - EXTRA) // 2
    shapes = [jax.ShapeDtypeStruct((tokens + TAIL, width), BF16)] * 2
    kernel = functools.partial(combine_kernel, at, rets.shape[0])
    extra = pl.BlockSpec((EXTRA, width), lambda *_: (2 * tokens // EXTRA, 0))
    specs = [extra, extra, whole(rets.shape)]
    return call(kernel, info, [mine, sibling, rets], shapes, specs)


def expert(at, info, msgs, weights, saved, chunk, chunks):
    sources = len(msgs)
    width = msgs[0].shape[1]
    hidden = weights[0].shape[2]
    tile = next(t for t in (256, 128) if hidden % t == 0)
    rows = sources * at.group
    gate_spec = pl.BlockSpec((1, width, tile), lambda f: (0, 0, f))
    down_t_spec = pl.BlockSpec((width, tile), lambda f: (0, f))
    up_t_spec = pl.BlockSpec((tile, width), lambda f: (f, 0))
    wide_spec = pl.BlockSpec(
        (rows, width), lambda f: (chunk, 0), pipeline_mode=pl.Buffered(1)
    )
    thin_spec = pl.BlockSpec((rows, tile), lambda f: (chunk, f))
    out_shape = [jax.ShapeDtypeStruct((sources, at.group, width), BF16)]
    out_specs = [whole(s.shape) for s in out_shape] + [wide_spec] * 2 + [thin_spec] * 3
    out_shape += [jax.ShapeDtypeStruct((chunks * rows, width), BF16)] * 2
    out_shape += [jax.ShapeDtypeStruct((chunks * rows, hidden), BF16)] * 3
    in_specs = [SMEM] + [whole(m.shape) for m in msgs] + [gate_spec] * 2 + [down_t_spec] + [up_t_spec] * 2
    aliases = {}
    if saved:
        aliases = {len(in_specs) + i: 1 + i for i in range(5)}
        in_specs += [pl.BlockSpec(memory_space=pl.ANY)] * 5
    out = pl.pallas_call(
        functools.partial(expert_kernel, at, sources, len(saved)),
        grid=(hidden // tile,),
        in_specs=in_specs,
        out_specs=out_specs,
        out_shape=out_shape,
        input_output_aliases=aliases,
        scratch_shapes=[
            pltpu.VMEM((rows, LANES), F32),
            pltpu.VMEM((rows, width), F32),
            pltpu.VMEM((rows, LANES), F32),
            pltpu.VMEM((rows + 8, tile), F32),
        ],
        compiler_params=params(30),
        cost_estimate=COST,
    )(info, *msgs, *weights, *saved)
    return out[0], out[1:]


def shards(tokens_x, grad_out, expert_ids, probs, w_gate, w_up, w_down):
    nodes, locals_ = lax.axis_size("node"), lax.axis_size("local")
    experts = nodes * locals_
    tokens, top = expert_ids.shape
    width = tokens_x.shape[1]
    at = Rows(tokens * top // experts + 1)
    node, local = lax.axis_index("node"), lax.axis_index("local")
    both = ("node", "local")
    chips = list(range(0, nodes, 2))
    targets = len(chips)

    def swap(value, dn=0, dz=0):
        pairs = [
            (n * locals_ + z, (n ^ dn) * locals_ + (z ^ dz))
            for n in range(nodes)
            for z in range(locals_)
        ]
        return lax.ppermute(value, both, pairs)

    same_core = [list(range(core, nodes, 2)) for core in range(2)]

    def back(value):
        return lax.all_to_all(
            value, "node", split_axis=0, concat_axis=0, axis_index_groups=same_core, tiled=True
        )

    def fence(*values):
        return lax.optimization_barrier(values)

    ids_t = expert_ids.T
    info = jnp.concatenate([local[None], node ^ jnp.array(chips, jnp.int32)]).astype(jnp.int32)
    payload = pack(tokens_x, grad_out, ids_t, probs.T.astype(F32), nodes, locals_)

    def sisters(block):
        return swap(block, 1)

    def fill(block, sister):
        return dispatch(at, targets, info, block, sister)

    def send(msgs):
        return [msgs[0]] + [swap(msgs[j], chips[j]) for j in range(1, targets)]

    def turn(token):
        down, gate, up, _ = fence(w_down, w_gate, w_up, token)
        return [w_gate, w_up, down[0].T, gate[0].T, up[0].T]

    def work(c, msgs, weights, saved):
        return expert(at, info, msgs, weights, saved, c, locals_)

    def merge(block, sister, ret):
        return combine(at, info, block, sister, ret)

    (go,) = fence(node < nodes)

    def at_once(step, *args):
        shapes = jax.eval_shape(step, *args)
        idle = lambda *_: jax.tree.map(lambda v: jnp.zeros(v.shape, v.dtype), shapes)
        return lax.cond(go, step, idle, *args)

    def prepare(block):
        def step(block):
            sister = sisters(block)
            return sister, fill(block, sister)

        return at_once(step, block)

    def home(parts):
        def step(keep, other):
            return (keep.astype(F32) + swap(other, 1).astype(F32)).astype(BF16)

        return at_once(step, *parts)

    def wgrad(a, b):
        return lax.dot_general(a, b, TN, preferred_element_type=F32).astype(BF16)

    if locals_ == 4:
        b0 = payload
        b1, b2 = swap(b0, 0, 1), swap(b0, 0, 2)
        s0, m0 = prepare(b0)
        p0 = send(m0)
        weights = turn(m0[0])
        b1, weights = fence(b1, weights)
        s1, m1 = prepare(b1)
        p0, m1 = fence(p0, m1)
        p1 = send(m1)
        s2, m2 = prepare(b2)
        p0, m2 = fence(p0, m2)
        r0, saved = work(0, p0, weights, ())
        p1, m2, b2, r0, saved = fence(p1, m2, b2, r0, saved)
        p2 = send(m2)
        b3 = swap(b2, 0, 1)
        r1, saved = work(1, p1, weights, saved)
        b3, r1 = fence(b3, r1)
        s3, m3 = prepare(b3)
        p2, m3, r1, saved = fence(p2, m3, r1, saved)
        p3 = send(m3)
        r1 = back(r1)
        r2, saved = work(2, p2, weights, saved)
        p3, r1, r2, saved = fence(p3, r1, r2, saved)
        r2 = back(r2)
        r3, saved = work(3, p3, weights, saved)
        r2, r3, r1, saved, r0 = fence(r2, r3, r1, saved, r0)
        t2 = home(merge(b2, s2, r2))
        t2, r3, r1, saved, r0 = fence(t2, r3, r1, saved, r0)
        r3 = back(r3)
        t2 = swap(t2, 0, 2)
        x_all, dy_all, hp, du, dg = saved
        t1 = home(merge(b1, s1, r1))
        gate_wgrad = wgrad(x_all, dg)
        r3, t1, r0, gate_wgrad = fence(r3, t1, r0, gate_wgrad)
        t3 = home(merge(b3, s3, r3))
        t3, r0, t1, x_all, dy_all, hp, du = fence(t3, r0, t1, x_all, dy_all, hp, du)
        t1 = swap(t1, 0, 1)
        t3 = swap(t3, 0, 3)
        r0 = back(r0)
        up_wgrad = wgrad(x_all, du)
        down_wgrad = wgrad(hp, dy_all)
        r0, up_wgrad, down_wgrad = fence(r0, up_wgrad, down_wgrad)
        t0 = home(merge(b0, s0, r0))
        t0, t1, t2, t3 = fence(t0, t1, t2, t3)
        totals = [t0, t1, t2, t3]
    else:
        weights, saved, totals = turn(payload), (), []
        for c in range(locals_):
            block = swap(payload, 0, c) if c else payload
            sister, msgs = prepare(block)
            ret, saved = work(c, send(msgs), weights, saved)
            total = home(merge(block, sister, back(ret)))
            totals.append(swap(total, 0, c) if c else total)
        x_all, dy_all, hp, du, dg = saved
        gate_wgrad, up_wgrad = wgrad(x_all, dg), wgrad(x_all, du)
        down_wgrad = wgrad(hp, dy_all)

    total = functools.reduce(
        lambda a, b: a + b, [totals[c][:tokens].astype(F32) for c in range(locals_)]
    )
    grad_x = total.astype(BF16)
    tails = jnp.stack([totals[c][tokens : tokens + 2, : targets * LANES] for c in range(locals_)])
    tails = tails.reshape(locals_, 2, targets, tokens)
    apart = ids_t ^ (node * locals_ + local)
    grad_probs = jnp.zeros((top, tokens), F32)
    for c in range(locals_):
        for dl in range(2):
            for j in range(targets):
                name = (chips[j] + dl) * locals_ + c
                grad_probs = jnp.where(apart == name, tails[c, dl, j].astype(F32)[None], grad_probs)
    grad_probs = grad_probs.T.astype(BF16)
    return (grad_x, grad_probs, gate_wgrad[None], up_wgrad[None], down_wgrad[None])


def solution(mesh):
    row, cube = P(("node", "local"), None), P(("node", "local"), None, None)
    return jax.shard_map(
        shards,
        mesh=mesh,
        in_specs=(row, row, row, row, cube, cube, cube),
        out_specs=(row, row, cube, cube, cube),
        check_vma=False,
    )
```

```python
import functools

import jax
import jax.numpy as jnp
from jax import lax
from jax.experimental import pallas as pl
from jax.experimental.pallas import tpu as pltpu
from jax.sharding import PartitionSpec as P

F32 = jnp.float32
BF16 = jnp.bfloat16
NT = (((1,), (1,)), ((), ()))
TN = (((0,), (0,)), ((), ()))
LANES = 128
EXTRA = 16
TAIL = 8


def pad_to(value, unit):
    return -(-value // unit) * unit


class Rows:
    def __init__(self, cap):
        self.slots = 2 * cap
        self.base = self.slots // 16 * 16
        self.shift = self.slots - self.base
        self.group = pad_to(self.slots + self.shift + 1, 8)
        self.prob = 2 * self.slots
        self.message = max(pad_to(self.prob + 1, 8), self.base + self.group)


def iota(shape, dim):
    return lax.broadcasted_iota(jnp.int32, shape, dim)


def eye(rows):
    return jnp.where(iota((rows, LANES), 0) == iota((rows, LANES), 1), 1.0, 0.0).astype(BF16)


def ranks(info_ref, w_refs, first, targets):
    place = iota((EXTRA, LANES), 0) == info_ref[0]
    lines = []
    for j in range(targets):
        lane = pl.multiple_of(info_ref[1 + j] * LANES, LANES)
        parts = []
        for w in w_refs:
            part = w[first : first + EXTRA, pl.ds(lane, LANES)].astype(F32)
            parts.append(jnp.sum(jnp.where(place, part, 0.0), axis=0, keepdims=True))
        lines.append(jnp.concatenate(parts, axis=1))
    tokens = lines[0].shape[1]
    lines.append(jnp.zeros((pad_to(targets, 8) - targets, tokens), F32))
    probs = jnp.concatenate([line for line in lines if line.shape[0]], axis=0)
    named = probs != 0.0
    upto = jnp.where(iota((tokens, tokens), 0) <= iota((tokens, tokens), 1), 1.0, 0.0).astype(BF16)
    count = jnp.dot(jnp.where(named, 1.0, 0.0).astype(BF16), upto, preferred_element_type=F32)
    return probs, jnp.where(named, count, -999.0)


def pick(rank, j, rows, start=0):
    slot = (iota((rows, rank.shape[1]), 0) + (1 - start)).astype(F32)
    return jnp.where(slot == rank[j : j + 1, :], 1.0, 0.0).astype(BF16)


def pack_kernel(nodes, locals_, x_ref, dy_ref, ids_ref, probs_ref, out_ref):
    tokens, width = x_ref.shape
    out_ref[:tokens, :] = x_ref[...]
    out_ref[tokens : 2 * tokens, :] = dy_ref[...]
    place = iota((EXTRA, tokens), 0)
    ids, probs = ids_ref[...], probs_ref[...].astype(F32)
    for n in range(width // tokens):
        line = jnp.zeros((EXTRA, tokens), F32)
        if n < nodes:
            for k in range(ids.shape[0]):
                hit = (place < locals_) & (ids[k : k + 1, :] == place + n * locals_)
                line = line + jnp.where(hit, probs[k : k + 1, :], 0.0)
        out_ref[2 * tokens :, n * tokens : (n + 1) * tokens] = line.astype(BF16)


def finish_kernel(chips, locals_, info_ref, ids_ref, *refs):
    totals, (grad_x_ref, grad_probs_ref) = refs[:-2], refs[-2:]
    tokens, width = grad_x_ref.shape
    step = next(s for s in (512, 256, 128) if width % s == 0)
    for start in range(0, width, step):
        cols = slice(start, start + step)
        total = totals[0][:tokens, cols].astype(F32)
        for t in totals[1:]:
            total = total + t[:tokens, cols].astype(F32)
        grad_x_ref[:, cols] = total.astype(BF16)
    apart = ids_ref[...] ^ info_ref[0]
    grads = jnp.zeros(apart.shape, F32)
    for c, t in enumerate(totals):
        for j, chip in enumerate(chips):
            tail = t[tokens:, j * LANES : (j + 1) * LANES].astype(F32)
            for dl in range(2):
                here = apart == (chip + dl) * locals_ + c
                grads = jnp.where(here, tail[dl : dl + 1, :], grads)
    grad_probs_ref[...] = grads.astype(BF16)


def dispatch_kernel(at, targets, info_ref, mine_ref, sibling_ref, *outs):
    tokens = (mine_ref.shape[0] - EXTRA) // 2
    width = mine_ref.shape[1]
    blocks = (mine_ref, sibling_ref)
    probs, rank = ranks(info_ref, blocks, 2 * tokens, targets)
    picks, lines = [], []
    for j in range(targets):
        x = pick(rank, j, at.message)
        dy = pick(rank, j, at.message, at.slots)
        picks.append(
            jnp.concatenate([x[:, :tokens], dy[:, :tokens], x[:, tokens:], dy[:, tokens:]], axis=1)
        )
        lines.append(
            lax.dot_general(
                probs.astype(BF16), pick(rank, j, LANES), NT, preferred_element_type=F32
            )[j : j + 1, :]
        )
    picks = jnp.concatenate(picks, axis=0)
    step = next(s for s in (1024, 512, 256, 128) if width % s == 0)
    for start in range(0, width, step):
        rows = jnp.concatenate([b[: 2 * tokens, start : start + step] for b in blocks], axis=0)
        out = jnp.dot(picks, rows, preferred_element_type=F32)
        for j in range(targets):
            part = out[j * at.message : (j + 1) * at.message]
            if start == 0:
                line = jnp.concatenate([lines[j], jnp.zeros((1, step - LANES), F32)], axis=1)
                part = jnp.where(iota(part.shape, 0) == at.prob, line, part)
            if len(outs) == targets:
                outs[j][:, start : start + step] = part.astype(BF16)
            else:
                outs[0][info_ref[1 + j] // 2, :, start : start + step] = part.astype(BF16)


def combine_kernel(at, targets, info_ref, mine_ref, sibling_ref, *refs):
    rets_ref, keep_ref, send_ref = refs
    chips = [info_ref[1 + j] // 2 for j in range(targets)]
    tokens = keep_ref.shape[0] - TAIL
    width = keep_ref.shape[1]
    _, rank = ranks(info_ref, (mine_ref, sibling_ref), 0, targets)
    picks = jnp.concatenate([pick(rank, j, at.group) for j in range(targets)], axis=0)
    step = next(s for s in (1024, 512, 256, 128) if width % s == 0)
    for start in range(0, width, step):
        rows = [rets_ref[chips[j], :, start : start + step] for j in range(targets)]
        total = lax.dot_general(
            picks, jnp.concatenate(rows, axis=0), TN, preferred_element_type=F32
        )
        keep_ref[:tokens, start : start + step] = total[:tokens].astype(BF16)
        send_ref[:tokens, start : start + step] = total[tokens:].astype(BF16)
    row = iota((TAIL, LANES), 0)
    for n in range(width // LANES):
        keep = send = jnp.zeros((TAIL, LANES), F32)
        if n < targets:
            tail = rets_ref[chips[n], at.group - 8 :, :LANES]
            line = jnp.dot(tail, pick(rank, n, LANES), preferred_element_type=F32)[7:8]
            keep = jnp.where(row == 0, line[:, :tokens], keep)
            send = jnp.where(row == 1, line[:, tokens:], send)
        keep_ref[tokens:, n * LANES : (n + 1) * LANES] = keep.astype(BF16)
        send_ref[tokens:, n * LANES : (n + 1) * LANES] = send.astype(BF16)


def expert_kernel(at, sources, aliased, info_ref, *refs):
    joined = len(refs[0].shape) == 3
    if joined:
        msgs, refs = [refs[0].at[i] for i in range(sources)], refs[1:]
    else:
        msgs, refs = refs[:sources], refs[sources:]
    stored, refs = refs[:5], refs[5 + aliased :]
    ret_ref, x_all, dy_all, hp_ref, du_ref, dg_ref = refs[:6]
    held, (moved_ref, sems) = refs[6:11], refs[11:]
    rows, hidden = hp_ref.shape
    width = x_all.shape[1]
    group, shift = at.group, at.shift
    copies = [
        pltpu.make_async_copy(src, dst, sems.at[i]) for i, (src, dst) in enumerate(zip(stored, held))
    ]
    for copy in copies:
        copy.start()
    x_all[...] = jnp.concatenate([m[:group, :] for m in msgs], axis=0)
    dy_all[...] = jnp.concatenate([m[at.base : at.base + group, :] for m in msgs], axis=0)
    first = at.prob // 8 * 8
    line = at.prob - first
    p = jnp.concatenate(
        [
            lax.dot_general(
                eye(group), m[first : first + 8, :LANES], NT, preferred_element_type=F32
            )[:, line : line + 1]
            for m in msgs
        ],
        axis=0,
    )
    copies[0].wait()
    g = jnp.dot(x_all[...], held[0][0], preferred_element_type=F32)
    copies[1].wait()
    u = jnp.dot(x_all[...], held[1][0], preferred_element_type=F32)
    copies[2].wait()
    moved_ref[:rows, :] = jnp.dot(dy_all[...], held[2][...], preferred_element_type=F32)
    moved_ref[rows:, :] = jnp.zeros((8, hidden), F32)
    dh = moved_ref[shift : shift + rows, :]
    s = jax.nn.sigmoid(g)
    a = g * s
    h = a * u
    sd = dh * p
    pg = jnp.sum(dh * h, axis=1, keepdims=True)
    du_ref[...] = (sd * a).astype(BF16)
    dg_ref[...] = (sd * u * s * (1.0 + g * (1.0 - s))).astype(BF16)
    moved_ref[:8, :] = jnp.zeros((8, hidden), F32)
    moved_ref[shift : shift + rows, :] = h * p
    hp_ref[...] = moved_ref[:rows, :].astype(BF16)
    pg = (pg + jnp.zeros((rows, LANES), F32)).astype(BF16)
    last = iota((8, LANES), 0) == 7
    copies[3].wait()
    copies[4].wait()
    step = next(s for s in (1024, 512, 256, 128) if width % s == 0)
    for start in range(0, width, step):
        cols = slice(start, start + step)
        dx = jnp.dot(dg_ref[...], held[3][:, cols], preferred_element_type=F32)
        dx = dx + jnp.dot(du_ref[...], held[4][:, cols], preferred_element_type=F32)
        for i in range(sources):
            chip = i if joined else info_ref[1 + i] // 2
            part = slice(i * group, (i + 1) * group)
            ret_ref[chip, :, cols] = dx[part, :].astype(BF16)
            if start == 0:
                grads = lax.dot_general(
                    pg[part, :], eye(group), TN, preferred_element_type=F32
                )[:1]
                tail = jnp.where(last, grads, dx[(i + 1) * group - 8 : (i + 1) * group, :LANES])
                ret_ref[chip, group - 8 :, :LANES] = tail.astype(BF16)


def whole(shape):
    return pl.BlockSpec(shape, lambda *_: (0,) * len(shape), pipeline_mode=pl.Buffered(1))


def params(mib):
    return pltpu.CompilerParams(vmem_limit_bytes=mib * 1024 * 1024)


COST = pl.CostEstimate(flops=1024, bytes_accessed=1024, transcendentals=0)


SMEM = pl.BlockSpec(memory_space=pltpu.SMEM)


def call(kernel, info, operands, out_shape, in_specs=None, mib=60):
    return pl.pallas_call(
        kernel,
        grid=(1,),
        in_specs=([SMEM] if info is not None else [])
        + (in_specs or [whole(a.shape) for a in operands]),
        out_specs=[whole(s.shape) for s in out_shape],
        out_shape=out_shape,
        compiler_params=params(mib),
        cost_estimate=COST,
    )(*([info] if info is not None else []), *operands)


def pack(x, dy, ids, probs, nodes, locals_):
    tokens, width = x.shape
    shape = jax.ShapeDtypeStruct((2 * tokens + EXTRA, width), BF16)
    kernel = functools.partial(pack_kernel, nodes, locals_)
    return call(kernel, None, [x, dy, ids, probs], [shape])[0]


def finish(info, ids_t, totals, chips, locals_):
    tokens, width = totals[0].shape[0] - TAIL, totals[0].shape[1]
    shapes = [
        jax.ShapeDtypeStruct((tokens, width), BF16),
        jax.ShapeDtypeStruct(ids_t.shape, BF16),
    ]
    kernel = functools.partial(finish_kernel, chips, locals_)
    grad_x, grad_probs = call(kernel, info, [ids_t, *totals], shapes, mib=24)
    return grad_x, grad_probs.T


def dispatch(at, targets, info, mine, sibling, joined):
    height, width = mine.shape
    if joined:
        shapes = [jax.ShapeDtypeStruct((targets, at.message, width), BF16)]
    else:
        shapes = [jax.ShapeDtypeStruct((at.message, width), BF16)] * targets
    kernel = functools.partial(dispatch_kernel, at, targets)
    out = call(kernel, info, [mine, sibling], shapes)
    return out[0] if joined else out


def combine(at, info, mine, sibling, rets):
    height, width = mine.shape
    tokens = (height - EXTRA) // 2
    shapes = [jax.ShapeDtypeStruct((tokens + TAIL, width), BF16)] * 2
    kernel = functools.partial(combine_kernel, at, rets.shape[0])
    extra = pl.BlockSpec((EXTRA, width), lambda *_: (2 * tokens // EXTRA, 0))
    specs = [extra, extra, whole(rets.shape)]
    return call(kernel, info, [mine, sibling, rets], shapes, specs, 24)


def expert(at, info, msgs, weights, saved, chunk, chunks):
    sources = sum(m.size // (at.message * m.shape[-1]) for m in msgs)
    width = msgs[0].shape[-1]
    hidden = weights[0].shape[2]
    rows = sources * at.group
    wide_spec, thin_spec = (
        pl.BlockSpec((rows, n), lambda *_: (chunk, 0), pipeline_mode=pl.Buffered(1))
        for n in (width, hidden)
    )
    out_shape = [jax.ShapeDtypeStruct((sources, at.group, width), BF16)]
    out_specs = [whole(s.shape) for s in out_shape] + [wide_spec] * 2 + [thin_spec] * 3
    out_shape += [jax.ShapeDtypeStruct((chunks * rows, width), BF16)] * 2
    out_shape += [jax.ShapeDtypeStruct((chunks * rows, hidden), BF16)] * 3
    in_specs = [SMEM] + [whole(m.shape) for m in msgs]
    in_specs += [pl.BlockSpec(memory_space=pl.ANY)] * (5 + len(saved))
    aliases = {1 + len(msgs) + 5 + i: 1 + i for i in range(len(saved))}
    out = pl.pallas_call(
        functools.partial(expert_kernel, at, sources, len(saved)),
        grid=(1,),
        in_specs=in_specs,
        out_specs=out_specs,
        out_shape=out_shape,
        input_output_aliases=aliases,
        scratch_shapes=[pltpu.VMEM(w.shape, BF16) for w in weights]
        + [pltpu.VMEM((rows + 8, hidden), F32), pltpu.SemaphoreType.DMA((5,))],
        compiler_params=params(60),
        cost_estimate=COST,
    )(info, *msgs, *weights, *saved)
    return out[0], out[1:]


def shards(tokens_x, grad_out, expert_ids, probs, w_gate, w_up, w_down):
    nodes, locals_ = lax.axis_size("node"), lax.axis_size("local")
    experts = nodes * locals_
    tokens, top = expert_ids.shape
    width = tokens_x.shape[1]
    at = Rows(tokens * top // experts + 1)
    node, local = lax.axis_index("node"), lax.axis_index("local")
    both = ("node", "local")
    chips = list(range(0, nodes, 2))
    targets = len(chips)

    def swap(value, dn=0, dz=0):
        pairs = [
            (n * locals_ + z, (n ^ dn) * locals_ + (z ^ dz))
            for n in range(nodes)
            for z in range(locals_)
        ]
        return lax.ppermute(value, both, pairs)

    def along(value, moves):
        pairs = [(n * locals_ + a, n * locals_ + b) for n in range(nodes) for a, b in moves]
        return lax.ppermute(value, both, pairs)

    middle = (local == 1) | (local == 2)
    same_core = [list(range(core, nodes, 2)) for core in range(2)]

    def back(value):
        return lax.all_to_all(
            value, "node", split_axis=0, concat_axis=0, axis_index_groups=same_core, tiled=True
        )

    def fence(*values):
        return lax.optimization_barrier(values)

    ids_t = expert_ids.T
    info = jnp.concatenate([local[None], node ^ jnp.array(chips, jnp.int32)]).astype(jnp.int32)
    payload = pack(tokens_x, grad_out, ids_t, probs.T, nodes, locals_)

    def sisters(block):
        return swap(block, 1)

    def fill(block, sister, joined):
        return dispatch(at, targets, info, block, sister, joined)

    def send(msgs):
        return [msgs[0]] + [swap(msgs[j], chips[j]) for j in range(1, targets)]

    def turn(token):
        down, gate, up, _ = fence(w_down, w_gate, w_up, token)
        return [w_gate, w_up, down[0].T, gate[0].T, up[0].T]

    def work(c, msgs, weights, saved):
        return expert(at, info, msgs, weights, saved, c, locals_)

    def merge(block, sister, ret):
        return combine(at, info, block, sister, ret)

    (go,) = fence(node < nodes)

    def at_once(step, *args):
        shapes = jax.eval_shape(step, *args)
        idle = lambda *_: jax.tree.map(lambda v: jnp.zeros(v.shape, v.dtype), shapes)
        return lax.cond(go, step, idle, *args)

    def prepare(block, joined=False):
        def step(block):
            sister = sisters(block)
            return sister, fill(block, sister, joined)

        return at_once(step, block)

    def home(parts):
        def step(keep, other):
            return (keep.astype(F32) + swap(other, 1).astype(F32)).astype(BF16)

        return at_once(step, *parts)

    def wgrad(a, b):
        return lax.dot_general(a, b, TN, preferred_element_type=F32).astype(BF16)

    if locals_ == 4:
        b0 = payload
        b1, inner = swap(b0, 0, 1), along(b0, [(1, 2), (2, 1)])
        s0, m0 = prepare(b0, joined=True)
        p0 = back(m0)
        weights = turn(m0)
        b1, inner, weights = fence(b1, inner, weights)
        outward, inner2 = along(inner, [(1, 0), (2, 3)]), along(b1, [(1, 2), (2, 1)])
        s1, m1 = prepare(b1)
        p0, m1 = fence(p0, m1)
        p1 = send(m1)
        r0, saved = work(0, [p0], weights, ())
        outward, inner2, r0 = fence(outward, inner2, r0)
        b2 = jnp.where(middle, inner2, outward)
        s2, m2 = prepare(b2)
        p1, m2, b2, r0, saved = fence(p1, m2, b2, r0, saved)
        p2 = send(m2)
        b3 = swap(b2, 0, 1)
        r1, saved = work(1, p1, weights, saved)
        b3, r1 = fence(b3, r1)
        s3, m3 = prepare(b3)
        p2, m3, r1, saved = fence(p2, m3, r1, saved)
        p3 = send(m3)
        r2, saved = work(2, p2, weights, saved)
        p3, r2, saved = fence(p3, r2, saved)
        r2 = back(r2)
        r3, saved = work(3, p3, weights, saved)
        r2, r3, saved = fence(r2, r3, saved)
        t2 = home(merge(b2, s2, r2))
        t2, r3, saved = fence(t2, r3, saved)
        r3 = back(r3)
        t2 = swap(t2, 0, 2)
        x_all, dy_all, hp, du, dg = saved
        gate_wgrad = wgrad(x_all, dg)
        r3, gate_wgrad = fence(r3, gate_wgrad)
        t3 = home(merge(b3, s3, r3))
        t3, r0, r1, x_all, dy_all, hp, du = fence(t3, r0, r1, x_all, dy_all, hp, du)
        t3 = swap(t3, 0, 3)
        r1 = back(r1)
        up_wgrad, down_wgrad = wgrad(x_all, du), wgrad(hp, dy_all)
        r1, r0, t2, up_wgrad, down_wgrad = fence(r1, r0, t2, up_wgrad, down_wgrad)
        r0 = back(r0)
        r1, t3 = fence(r1, t3)
        t1 = swap(home(merge(b1, s1, r1)), 0, 1)
        t0 = home(merge(b0, s0, r0))
        t0, t1, t2, t3 = fence(t0, t1, t2, t3)
        totals = [t0, t1, t2, t3]
    else:
        weights, saved, totals = turn(payload), (), []
        for c in range(locals_):
            block = swap(payload, 0, c) if c else payload
            sister, msgs = prepare(block)
            ret, saved = work(c, send(msgs), weights, saved)
            total = home(merge(block, sister, back(ret)))
            totals.append(swap(total, 0, c) if c else total)
        x_all, dy_all, hp, du, dg = saved
        gate_wgrad, up_wgrad = wgrad(x_all, dg), wgrad(x_all, du)
        down_wgrad = wgrad(hp, dy_all)

    me = (node * locals_ + local)[None].astype(jnp.int32)
    grad_x, grad_probs = finish(me, ids_t, totals, chips, locals_)
    return (grad_x, grad_probs, gate_wgrad[None], up_wgrad[None], down_wgrad[None])


def solution(mesh):
    row, cube = P(("node", "local"), None), P(("node", "local"), None, None)
    return jax.shard_map(
        shards,
        mesh=mesh,
        in_specs=(row, row, row, row, cube, cube, cube),
        out_specs=(row, row, cube, cube, cube),
        check_vma=False,
    )
```

```python
import functools

import jax
import jax.numpy as jnp
from jax import lax
from jax.experimental import pallas as pl
from jax.experimental.pallas import tpu as pltpu
from jax.sharding import PartitionSpec as P

F32 = jnp.float32
BF16 = jnp.bfloat16
NT = (((1,), (1,)), ((), ()))
TN = (((0,), (0,)), ((), ()))
LANES = 128
EXTRA = 16
TAIL = 8


def pad_to(value, unit):
    return -(-value // unit) * unit


class Rows:
    def __init__(self, cap):
        self.slots = 2 * cap
        self.base = self.slots // 16 * 16
        self.shift = self.slots - self.base
        self.group = pad_to(self.slots + self.shift + 1, 8)
        self.prob = 2 * self.slots
        self.message = max(pad_to(self.prob + 1, 8), self.base + self.group)


def iota(shape, dim):
    return lax.broadcasted_iota(jnp.int32, shape, dim)


def eye(rows):
    return jnp.where(iota((rows, LANES), 0) == iota((rows, LANES), 1), 1.0, 0.0).astype(BF16)


def ranks(info_ref, w_refs, first, targets):
    place = iota((EXTRA, LANES), 0) == info_ref[0]
    lines = []
    for j in range(targets):
        lane = pl.multiple_of(info_ref[1 + j] * LANES, LANES)
        parts = []
        for w in w_refs:
            part = w[first : first + EXTRA, pl.ds(lane, LANES)].astype(F32)
            parts.append(jnp.sum(jnp.where(place, part, 0.0), axis=0, keepdims=True))
        lines.append(jnp.concatenate(parts, axis=1))
    tokens = lines[0].shape[1]
    lines.append(jnp.zeros((pad_to(targets, 8) - targets, tokens), F32))
    probs = jnp.concatenate([line for line in lines if line.shape[0]], axis=0)
    named = probs != 0.0
    upto = jnp.where(iota((tokens, tokens), 0) <= iota((tokens, tokens), 1), 1.0, 0.0).astype(BF16)
    count = jnp.dot(jnp.where(named, 1.0, 0.0).astype(BF16), upto, preferred_element_type=F32)
    return probs, jnp.where(named, count, -999.0)


def pick(rank, j, rows, start=0):
    slot = (iota((rows, rank.shape[1]), 0) + (1 - start)).astype(F32)
    return jnp.where(slot == rank[j : j + 1, :], 1.0, 0.0).astype(BF16)


def pack_kernel(nodes, locals_, x_ref, dy_ref, ids_ref, probs_ref, out_ref):
    tokens, width = x_ref.shape
    out_ref[:tokens, :] = x_ref[...]
    out_ref[tokens : 2 * tokens, :] = dy_ref[...]
    place = iota((EXTRA, tokens), 0)
    ids, probs = ids_ref[...], probs_ref[...].astype(F32)
    for n in range(width // tokens):
        line = jnp.zeros((EXTRA, tokens), F32)
        if n < nodes:
            for k in range(ids.shape[0]):
                hit = (place < locals_) & (ids[k : k + 1, :] == place + n * locals_)
                line = line + jnp.where(hit, probs[k : k + 1, :], 0.0)
        out_ref[2 * tokens :, n * tokens : (n + 1) * tokens] = line.astype(BF16)


def finish_kernel(chips, locals_, info_ref, ids_ref, *refs):
    totals, (grad_x_ref, grad_probs_ref) = refs[:-2], refs[-2:]
    tokens, width = grad_x_ref.shape
    step = next(s for s in (512, 256, 128) if width % s == 0)
    for start in range(0, width, step):
        cols = slice(start, start + step)
        total = totals[0][:tokens, cols].astype(F32)
        for t in totals[1:]:
            total = total + t[:tokens, cols].astype(F32)
        grad_x_ref[:, cols] = total.astype(BF16)
    apart = ids_ref[...] ^ info_ref[0]
    grads = jnp.zeros(apart.shape, F32)
    for c, t in enumerate(totals):
        for j, chip in enumerate(chips):
            tail = t[tokens:, j * LANES : (j + 1) * LANES].astype(F32)
            for dl in range(2):
                here = apart == (chip + dl) * locals_ + c
                grads = jnp.where(here, tail[dl : dl + 1, :], grads)
    grad_probs_ref[...] = grads.astype(BF16)


def dispatch_kernel(at, targets, info_ref, mine_ref, sibling_ref, *outs):
    tokens = (mine_ref.shape[0] - EXTRA) // 2
    width = mine_ref.shape[1]
    blocks = (mine_ref, sibling_ref)
    probs, rank = ranks(info_ref, blocks, 2 * tokens, targets)
    picks, lines = [], []
    for j in range(targets):
        x = pick(rank, j, at.message)
        dy = pick(rank, j, at.message, at.slots)
        picks.append(
            jnp.concatenate([x[:, :tokens], dy[:, :tokens], x[:, tokens:], dy[:, tokens:]], axis=1)
        )
        lines.append(
            lax.dot_general(
                probs.astype(BF16), pick(rank, j, LANES), NT, preferred_element_type=F32
            )[j : j + 1, :]
        )
    picks = jnp.concatenate(picks, axis=0)
    step = next(s for s in (1024, 512, 256, 128) if width % s == 0)
    for start in range(0, width, step):
        rows = jnp.concatenate([b[: 2 * tokens, start : start + step] for b in blocks], axis=0)
        out = jnp.dot(picks, rows, preferred_element_type=F32)
        for j in range(targets):
            part = out[j * at.message : (j + 1) * at.message]
            if start == 0:
                line = jnp.concatenate([lines[j], jnp.zeros((1, step - LANES), F32)], axis=1)
                part = jnp.where(iota(part.shape, 0) == at.prob, line, part)
            if len(outs) == targets:
                outs[j][:, start : start + step] = part.astype(BF16)
            else:
                outs[0][info_ref[1 + j] // 2, :, start : start + step] = part.astype(BF16)


def combine_kernel(at, targets, info_ref, mine_ref, sibling_ref, *refs):
    rets_ref, keep_ref, send_ref = refs
    chips = [info_ref[1 + j] // 2 for j in range(targets)]
    tokens = keep_ref.shape[0] - TAIL
    width = keep_ref.shape[1]
    _, rank = ranks(info_ref, (mine_ref, sibling_ref), 0, targets)
    picks = jnp.concatenate([pick(rank, j, at.group) for j in range(targets)], axis=0)
    step = next(s for s in (1024, 512, 256, 128) if width % s == 0)
    for start in range(0, width, step):
        rows = [rets_ref[chips[j], 0, :, start : start + step] for j in range(targets)]
        total = lax.dot_general(
            picks, jnp.concatenate(rows, axis=0), TN, preferred_element_type=F32
        )
        keep_ref[:tokens, start : start + step] = total[:tokens].astype(BF16)
        send_ref[:tokens, start : start + step] = total[tokens:].astype(BF16)
    row = iota((TAIL, LANES), 0)
    for n in range(width // LANES):
        keep = send = jnp.zeros((TAIL, LANES), F32)
        if n < targets:
            tail = rets_ref[chips[n], 0, at.group - 8 :, :LANES]
            line = jnp.dot(tail, pick(rank, n, LANES), preferred_element_type=F32)[7:8]
            keep = jnp.where(row == 0, line[:, :tokens], keep)
            send = jnp.where(row == 1, line[:, tokens:], send)
        keep_ref[tokens:, n * LANES : (n + 1) * LANES] = keep.astype(BF16)
        send_ref[tokens:, n * LANES : (n + 1) * LANES] = send.astype(BF16)


def expert_kernel(at, sources, aliased, info_ref, *refs):
    joined = len(refs[0].shape) == 3
    if joined:
        msgs, refs = [refs[0].at[i] for i in range(sources)], refs[1:]
    else:
        msgs, refs = refs[:sources], refs[sources:]
    stored, refs = refs[:5], refs[5 + aliased :]
    ret_ref, x_all, dy_all, hp_ref, du_ref, dg_ref = refs[:6]
    held, (moved_ref, sems) = refs[6:11], refs[11:]
    rows, hidden = hp_ref.shape
    width = x_all.shape[1]
    group, shift = at.group, at.shift
    copies = [
        pltpu.make_async_copy(src, dst, sems.at[i]) for i, (src, dst) in enumerate(zip(stored, held))
    ]
    for copy in copies:
        copy.start()
    x_all[...] = jnp.concatenate([m[:group, :] for m in msgs], axis=0)
    dy_all[...] = jnp.concatenate([m[at.base : at.base + group, :] for m in msgs], axis=0)
    first = at.prob // 8 * 8
    line = at.prob - first
    p = jnp.concatenate(
        [
            lax.dot_general(
                eye(group), m[first : first + 8, :LANES], NT, preferred_element_type=F32
            )[:, line : line + 1]
            for m in msgs
        ],
        axis=0,
    )
    copies[0].wait()
    g = jnp.dot(x_all[...], held[0][0], preferred_element_type=F32)
    copies[1].wait()
    u = jnp.dot(x_all[...], held[1][0], preferred_element_type=F32)
    copies[2].wait()
    moved_ref[:rows, :] = jnp.dot(dy_all[...], held[2][...], preferred_element_type=F32)
    moved_ref[rows:, :] = jnp.zeros((8, hidden), F32)
    dh = moved_ref[shift : shift + rows, :]
    s = jax.nn.sigmoid(g)
    a = g * s
    h = a * u
    sd = dh * p
    pg = jnp.sum(dh * h, axis=1, keepdims=True)
    du_ref[...] = (sd * a).astype(BF16)
    dg_ref[...] = (sd * u * s * (1.0 + g * (1.0 - s))).astype(BF16)
    moved_ref[:8, :] = jnp.zeros((8, hidden), F32)
    moved_ref[shift : shift + rows, :] = h * p
    hp_ref[...] = moved_ref[:rows, :].astype(BF16)
    pg = (pg + jnp.zeros((rows, LANES), F32)).astype(BF16)
    last = iota((8, LANES), 0) == 7
    copies[3].wait()
    copies[4].wait()
    step = next(s for s in (1024, 512, 256, 128) if width % s == 0)
    for start in range(0, width, step):
        cols = slice(start, start + step)
        dx = jnp.dot(dg_ref[...], held[3][:, cols], preferred_element_type=F32)
        dx = dx + jnp.dot(du_ref[...], held[4][:, cols], preferred_element_type=F32)
        for i in range(sources):
            chip = i if joined else info_ref[1 + i] // 2
            part = slice(i * group, (i + 1) * group)
            ret_ref[chip, 0, :, cols] = dx[part, :].astype(BF16)
            if start == 0:
                grads = lax.dot_general(
                    pg[part, :], eye(group), TN, preferred_element_type=F32
                )[:1]
                tail = jnp.where(last, grads, dx[(i + 1) * group - 8 : (i + 1) * group, :LANES])
                ret_ref[chip, 0, group - 8 :, :LANES] = tail.astype(BF16)


def whole(shape):
    return pl.BlockSpec(shape, lambda *_: (0,) * len(shape), pipeline_mode=pl.Buffered(1))


def params(mib):
    return pltpu.CompilerParams(vmem_limit_bytes=mib * 1024 * 1024)


COST = pl.CostEstimate(flops=1024, bytes_accessed=1024, transcendentals=0)


SMEM = pl.BlockSpec(memory_space=pltpu.SMEM)


def call(kernel, info, operands, out_shape, in_specs=None, mib=60):
    return pl.pallas_call(
        kernel,
        grid=(1,),
        in_specs=([SMEM] if info is not None else [])
        + (in_specs or [whole(a.shape) for a in operands]),
        out_specs=[whole(s.shape) for s in out_shape],
        out_shape=out_shape,
        compiler_params=params(mib),
        cost_estimate=COST,
    )(*([info] if info is not None else []), *operands)


def pack(x, dy, ids, probs, nodes, locals_):
    tokens, width = x.shape
    shape = jax.ShapeDtypeStruct((2 * tokens + EXTRA, width), BF16)
    kernel = functools.partial(pack_kernel, nodes, locals_)
    return call(kernel, None, [x, dy, ids, probs], [shape])[0]


def finish(info, ids_t, totals, chips, locals_):
    tokens, width = totals[0].shape[0] - TAIL, totals[0].shape[1]
    shapes = [
        jax.ShapeDtypeStruct((tokens, width), BF16),
        jax.ShapeDtypeStruct(ids_t.shape, BF16),
    ]
    kernel = functools.partial(finish_kernel, chips, locals_)
    grad_x, grad_probs = call(kernel, info, [ids_t, *totals], shapes, mib=24)
    return grad_x, grad_probs.T


def dispatch(at, targets, info, mine, sibling, joined):
    height, width = mine.shape
    if joined:
        shapes = [jax.ShapeDtypeStruct((targets, at.message, width), BF16)]
    else:
        shapes = [jax.ShapeDtypeStruct((at.message, width), BF16)] * targets
    kernel = functools.partial(dispatch_kernel, at, targets)
    out = call(kernel, info, [mine, sibling], shapes)
    return out[0] if joined else out


def combine(at, info, mine, sibling, rets, slot):
    height, width = mine.shape
    tokens = (height - EXTRA) // 2
    shapes = [jax.ShapeDtypeStruct((tokens + TAIL, width), BF16)] * 2
    kernel = functools.partial(combine_kernel, at, rets.shape[0])
    extra = pl.BlockSpec((EXTRA, width), lambda *_: (2 * tokens // EXTRA, 0))
    targets, _, group, _ = rets.shape
    ret = pl.BlockSpec(
        (targets, 1, group, width), lambda *_: (0, slot, 0, 0), pipeline_mode=pl.Buffered(1)
    )
    specs = [extra, extra, ret]
    return call(kernel, info, [mine, sibling, rets], shapes, specs, 24)


def expert(at, info, msgs, weights, saved, chunk, chunks, slot, slots, ret):
    sources = sum(m.size // (at.message * m.shape[-1]) for m in msgs)
    width = msgs[0].shape[-1]
    hidden = weights[0].shape[2]
    rows = sources * at.group
    wide_spec, thin_spec = (
        pl.BlockSpec((rows, n), lambda *_: (chunk, 0), pipeline_mode=pl.Buffered(1))
        for n in (width, hidden)
    )
    out_shape = [jax.ShapeDtypeStruct((sources, slots, at.group, width), BF16)]
    ret_spec = pl.BlockSpec(
        (sources, 1, at.group, width), lambda *_: (0, slot, 0, 0), pipeline_mode=pl.Buffered(1)
    )
    out_specs = [ret_spec] + [wide_spec] * 2 + [thin_spec] * 3
    out_shape += [jax.ShapeDtypeStruct((chunks * rows, width), BF16)] * 2
    out_shape += [jax.ShapeDtypeStruct((chunks * rows, hidden), BF16)] * 3
    in_specs = [SMEM] + [whole(m.shape) for m in msgs]
    first = 1 + len(msgs) + 5
    aliases = {first + i: 1 + i for i in range(len(saved))}
    kept = list(saved)
    if ret is not None:
        aliases[first + len(saved)] = 0
        kept.append(ret)
    in_specs += [pl.BlockSpec(memory_space=pl.ANY)] * (5 + len(kept))
    out = pl.pallas_call(
        functools.partial(expert_kernel, at, sources, len(kept)),
        grid=(1,),
        in_specs=in_specs,
        out_specs=out_specs,
        out_shape=out_shape,
        input_output_aliases=aliases,
        scratch_shapes=[pltpu.VMEM(w.shape, BF16) for w in weights]
        + [pltpu.VMEM((rows + 8, hidden), F32), pltpu.SemaphoreType.DMA((5,))],
        compiler_params=params(60),
        cost_estimate=COST,
    )(info, *msgs, *weights, *kept)
    return out[0], out[1:]


def shards(tokens_x, grad_out, expert_ids, probs, w_gate, w_up, w_down):
    nodes, locals_ = lax.axis_size("node"), lax.axis_size("local")
    experts = nodes * locals_
    tokens, top = expert_ids.shape
    width = tokens_x.shape[1]
    at = Rows(tokens * top // experts + 1)
    node, local = lax.axis_index("node"), lax.axis_index("local")
    both = ("node", "local")
    chips = list(range(0, nodes, 2))
    targets = len(chips)

    def swap(value, dn=0, dz=0):
        pairs = [
            (n * locals_ + z, (n ^ dn) * locals_ + (z ^ dz))
            for n in range(nodes)
            for z in range(locals_)
        ]
        return lax.ppermute(value, both, pairs)

    def along(value, moves):
        pairs = [(n * locals_ + a, n * locals_ + b) for n in range(nodes) for a, b in moves]
        return lax.ppermute(value, both, pairs)

    middle = (local == 1) | (local == 2)
    same_core = [list(range(core, nodes, 2)) for core in range(2)]

    def back(value):
        return lax.all_to_all(
            value, "node", split_axis=0, concat_axis=0, axis_index_groups=same_core, tiled=True
        )

    def fence(*values):
        return lax.optimization_barrier(values)

    ids_t = expert_ids.T
    info = jnp.concatenate([local[None], node ^ jnp.array(chips, jnp.int32)]).astype(jnp.int32)
    payload = pack(tokens_x, grad_out, ids_t, probs.T, nodes, locals_)

    def sisters(block):
        return swap(block, 1)

    def fill(block, sister, joined):
        return dispatch(at, targets, info, block, sister, joined)

    def send(msgs):
        return [msgs[0]] + [swap(msgs[j], chips[j]) for j in range(1, targets)]

    def turn(token):
        down, gate, up, _ = fence(w_down, w_gate, w_up, token)
        return [w_gate, w_up, down[0].T, gate[0].T, up[0].T]

    def work(c, msgs, weights, saved, slot=0, slots=1, ret=None):
        return expert(at, info, msgs, weights, saved, c, locals_, slot, slots, ret)

    def merge(block, sister, ret, slot=0):
        return combine(at, info, block, sister, ret, slot)

    (go,) = fence(node < nodes)

    def at_once(step, *args):
        shapes = jax.eval_shape(step, *args)
        idle = lambda *_: jax.tree.map(lambda v: jnp.zeros(v.shape, v.dtype), shapes)
        return lax.cond(go, step, idle, *args)

    def prepare(block, joined=False):
        def step(block):
            sister = sisters(block)
            return sister, fill(block, sister, joined)

        return at_once(step, block)

    def home(*parts):
        def step(parts):
            moved = [swap(other, 1) for _, other in parts]
            return [
                (keep.astype(F32) + other.astype(F32)).astype(BF16)
                for (keep, _), other in zip(parts, moved)
            ]

        return at_once(step, parts)

    def wgrad(a, b):
        return lax.dot_general(a, b, TN, preferred_element_type=F32).astype(BF16)

    if locals_ == 4:
        b0 = payload
        b1, inner = swap(b0, 0, 1), along(b0, [(1, 2), (2, 1)])
        s0, m0 = prepare(b0, joined=True)
        p0 = back(m0)
        weights = turn(m0)
        b1, inner, weights = fence(b1, inner, weights)
        outward, inner2 = along(inner, [(1, 0), (2, 3)]), along(b1, [(1, 2), (2, 1)])
        s1, m1 = prepare(b1)
        p0, m1 = fence(p0, m1)
        p1 = send(m1)
        r0, saved = work(0, [p0], weights, ())
        outward, inner2, r0 = fence(outward, inner2, r0)
        b2 = jnp.where(middle, inner2, outward)
        s2, m2 = prepare(b2)
        p1, m2, b2, r0, saved = fence(p1, m2, b2, r0, saved)
        p2 = send(m2)
        b3 = swap(b2, 0, 1)
        r1, saved = work(1, p1, weights, saved, 0, 2)
        b3, r1 = fence(b3, r1)
        s3, m3 = prepare(b3)
        p2, m3, r1, saved = fence(p2, m3, r1, saved)
        p3 = send(m3)
        r2, saved = work(2, p2, weights, saved)
        p3, r2, saved = fence(p3, r2, saved)
        r2 = back(r2)
        r13, saved = work(3, p3, weights, saved, 1, 2, r1)
        r2, r13, saved = fence(r2, r13, saved)
        (t2,) = home(merge(b2, s2, r2))
        t2, r13, saved = fence(t2, r13, saved)
        r13 = back(r13)
        t2 = swap(t2, 0, 2)
        x_all, dy_all, hp, du, dg = saved
        gate_wgrad, up_wgrad = wgrad(x_all, dg), wgrad(x_all, du)
        r13, gate_wgrad, up_wgrad = fence(r13, gate_wgrad, up_wgrad)
        t3, t1 = home(merge(b3, s3, r13, 1), merge(b1, s1, r13, 0))
        t3, t1, t2, r0, dy_all, hp = fence(t3, t1, t2, r0, dy_all, hp)
        t3 = swap(t3, 0, 3)
        t1 = swap(t1, 0, 1)
        r0 = back(r0)
        down_wgrad = wgrad(hp, dy_all)
        r0, down_wgrad = fence(r0, down_wgrad)
        (t0,) = home(merge(b0, s0, r0))
        t0, t1, t2, t3 = fence(t0, t1, t2, t3)
        totals = [t0, t1, t2, t3]
    else:
        weights, saved, totals = turn(payload), (), []
        for c in range(locals_):
            block = swap(payload, 0, c) if c else payload
            sister, msgs = prepare(block)
            ret, saved = work(c, send(msgs), weights, saved)
            (total,) = home(merge(block, sister, back(ret)))
            totals.append(swap(total, 0, c) if c else total)
        x_all, dy_all, hp, du, dg = saved
        gate_wgrad, up_wgrad = wgrad(x_all, dg), wgrad(x_all, du)
        down_wgrad = wgrad(hp, dy_all)

    me = (node * locals_ + local)[None].astype(jnp.int32)
    grad_x, grad_probs = finish(me, ids_t, totals, chips, locals_)
    return (grad_x, grad_probs, gate_wgrad[None], up_wgrad[None], down_wgrad[None])


def solution(mesh):
    row, cube = P(("node", "local"), None), P(("node", "local"), None, None)
    return jax.shard_map(
        shards,
        mesh=mesh,
        in_specs=(row, row, row, row, cube, cube, cube),
        out_specs=(row, row, cube, cube, cube),
        check_vma=False,
    )
```

```python
import functools

import jax
import jax.numpy as jnp
from jax import lax
from jax.experimental import pallas as pl
from jax.experimental.pallas import tpu as pltpu
from jax.sharding import PartitionSpec as P

F32 = jnp.float32
BF16 = jnp.bfloat16
NT = (((1,), (1,)), ((), ()))
TN = (((0,), (0,)), ((), ()))
LANES = 128
EXTRA = 16
TAIL = 8


def pad_to(value, unit):
    return -(-value // unit) * unit


class Rows:
    def __init__(self, cap):
        self.slots = 2 * cap
        self.base = self.slots // 16 * 16
        self.shift = self.slots - self.base
        self.group = pad_to(self.slots + self.shift + 1, 8)
        self.prob = 2 * self.slots
        self.message = max(pad_to(self.prob + 1, 8), self.base + self.group)


def iota(shape, dim):
    return lax.broadcasted_iota(jnp.int32, shape, dim)


def eye(rows):
    return jnp.where(iota((rows, LANES), 0) == iota((rows, LANES), 1), 1.0, 0.0).astype(BF16)


def ranks(info_ref, w_refs, first, targets):
    place = iota((EXTRA, LANES), 0) == info_ref[0]
    lines = []
    for j in range(targets):
        lane = pl.multiple_of(info_ref[1 + j] * LANES, LANES)
        parts = []
        for w in w_refs:
            part = w[first : first + EXTRA, pl.ds(lane, LANES)].astype(F32)
            parts.append(jnp.sum(jnp.where(place, part, 0.0), axis=0, keepdims=True))
        lines.append(jnp.concatenate(parts, axis=1))
    tokens = lines[0].shape[1]
    lines.append(jnp.zeros((pad_to(targets, 8) - targets, tokens), F32))
    probs = jnp.concatenate([line for line in lines if line.shape[0]], axis=0)
    named = probs != 0.0
    upto = jnp.where(iota((tokens, tokens), 0) <= iota((tokens, tokens), 1), 1.0, 0.0).astype(BF16)
    count = jnp.dot(jnp.where(named, 1.0, 0.0).astype(BF16), upto, preferred_element_type=F32)
    return probs, jnp.where(named, count, -999.0)


def pick(rank, j, rows, start=0):
    slot = (iota((rows, rank.shape[1]), 0) + (1 - start)).astype(F32)
    return jnp.where(slot == rank[j : j + 1, :], 1.0, 0.0).astype(BF16)


def pack_kernel(nodes, locals_, x_ref, dy_ref, ids_ref, probs_ref, out_ref):
    tokens, width = x_ref.shape
    out_ref[:tokens, :] = x_ref[...]
    out_ref[tokens : 2 * tokens, :] = dy_ref[...]
    place = iota((EXTRA, tokens), 0)
    ids, probs = ids_ref[...], probs_ref[...].astype(F32)
    for n in range(width // tokens):
        line = jnp.zeros((EXTRA, tokens), F32)
        if n < nodes:
            for k in range(ids.shape[0]):
                hit = (place < locals_) & (ids[k : k + 1, :] == place + n * locals_)
                line = line + jnp.where(hit, probs[k : k + 1, :], 0.0)
        out_ref[2 * tokens :, n * tokens : (n + 1) * tokens] = line.astype(BF16)


def finish_kernel(chips, locals_, info_ref, ids_ref, *refs):
    totals, (grad_x_ref, grad_probs_ref) = refs[:-2], refs[-2:]
    tokens, width = grad_x_ref.shape
    step = next(s for s in (512, 256, 128) if width % s == 0)
    for start in range(0, width, step):
        cols = slice(start, start + step)
        total = totals[0][:tokens, cols].astype(F32)
        for t in totals[1:]:
            total = total + t[:tokens, cols].astype(F32)
        grad_x_ref[:, cols] = total.astype(BF16)
    apart = ids_ref[...] ^ info_ref[0]
    grads = jnp.zeros(apart.shape, F32)
    for c, t in enumerate(totals):
        for j, chip in enumerate(chips):
            tail = t[tokens:, j * LANES : (j + 1) * LANES].astype(F32)
            for dl in range(2):
                here = apart == (chip + dl) * locals_ + c
                grads = jnp.where(here, tail[dl : dl + 1, :], grads)
    grad_probs_ref[...] = grads.astype(BF16)


def dispatch_kernel(at, targets, info_ref, mine_ref, sibling_ref, *outs):
    tokens = (mine_ref.shape[0] - EXTRA) // 2
    width = mine_ref.shape[1]
    blocks = (mine_ref, sibling_ref)
    probs, rank = ranks(info_ref, blocks, 2 * tokens, targets)
    picks, lines = [], []
    for j in range(targets):
        x = pick(rank, j, at.message)
        dy = pick(rank, j, at.message, at.slots)
        picks.append(
            jnp.concatenate([x[:, :tokens], dy[:, :tokens], x[:, tokens:], dy[:, tokens:]], axis=1)
        )
        lines.append(
            lax.dot_general(
                probs.astype(BF16), pick(rank, j, LANES), NT, preferred_element_type=F32
            )[j : j + 1, :]
        )
    picks = jnp.concatenate(picks, axis=0)
    step = next(s for s in (1024, 512, 256, 128) if width % s == 0)
    for start in range(0, width, step):
        rows = jnp.concatenate([b[: 2 * tokens, start : start + step] for b in blocks], axis=0)
        out = jnp.dot(picks, rows, preferred_element_type=F32)
        for j in range(targets):
            part = out[j * at.message : (j + 1) * at.message]
            if start == 0:
                line = jnp.concatenate([lines[j], jnp.zeros((1, step - LANES), F32)], axis=1)
                part = jnp.where(iota(part.shape, 0) == at.prob, line, part)
            if len(outs) == targets:
                outs[j][:, start : start + step] = part.astype(BF16)
            else:
                outs[0][info_ref[1 + j] // 2, :, start : start + step] = part.astype(BF16)


def combine_kernel(at, targets, info_ref, mine_ref, sibling_ref, *refs):
    rets_ref, keep_ref, send_ref = refs
    chips = [info_ref[1 + j] // 2 for j in range(targets)]
    tokens = keep_ref.shape[0] - TAIL
    width = keep_ref.shape[1]
    _, rank = ranks(info_ref, (mine_ref, sibling_ref), 0, targets)
    picks = jnp.concatenate([pick(rank, j, at.group) for j in range(targets)], axis=0)
    step = next(s for s in (1024, 512, 256, 128) if width % s == 0)
    for start in range(0, width, step):
        rows = [rets_ref[chips[j], 0, :, start : start + step] for j in range(targets)]
        total = lax.dot_general(
            picks, jnp.concatenate(rows, axis=0), TN, preferred_element_type=F32
        )
        keep_ref[:tokens, start : start + step] = total[:tokens].astype(BF16)
        send_ref[:tokens, start : start + step] = total[tokens:].astype(BF16)
    row = iota((TAIL, LANES), 0)
    for n in range(width // LANES):
        keep = send = jnp.zeros((TAIL, LANES), F32)
        if n < targets:
            tail = rets_ref[chips[n], 0, at.group - 8 :, :LANES]
            line = jnp.dot(tail, pick(rank, n, LANES), preferred_element_type=F32)[7:8]
            keep = jnp.where(row == 0, line[:, :tokens], keep)
            send = jnp.where(row == 1, line[:, tokens:], send)
        keep_ref[tokens:, n * LANES : (n + 1) * LANES] = keep.astype(BF16)
        send_ref[tokens:, n * LANES : (n + 1) * LANES] = send.astype(BF16)


def expert_kernel(at, sources, aliased, info_ref, *refs):
    joined = len(refs[0].shape) == 3
    if joined:
        msgs, refs = [refs[0].at[i] for i in range(sources)], refs[1:]
    else:
        msgs, refs = refs[:sources], refs[sources:]
    stored, refs = refs[:5], refs[5 + aliased :]
    ret_ref, x_all, dy_all, hp_ref, du_ref, dg_ref = refs[:6]
    held, (moved_ref, sems) = refs[6:11], refs[11:]
    rows, hidden = hp_ref.shape
    width = x_all.shape[1]
    group, shift = at.group, at.shift
    copies = [
        pltpu.make_async_copy(src, dst, sems.at[i]) for i, (src, dst) in enumerate(zip(stored, held))
    ]
    for copy in copies:
        copy.start()
    x_all[...] = jnp.concatenate([m[:group, :] for m in msgs], axis=0)
    dy_all[...] = jnp.concatenate([m[at.base : at.base + group, :] for m in msgs], axis=0)
    first = at.prob // 8 * 8
    line = at.prob - first
    p = jnp.concatenate(
        [
            lax.dot_general(
                eye(group), m[first : first + 8, :LANES], NT, preferred_element_type=F32
            )[:, line : line + 1]
            for m in msgs
        ],
        axis=0,
    )
    copies[0].wait()
    g = jnp.dot(x_all[...], held[0][0], preferred_element_type=F32)
    copies[1].wait()
    u = jnp.dot(x_all[...], held[1][0], preferred_element_type=F32)
    copies[2].wait()
    moved_ref[:rows, :] = jnp.dot(dy_all[...], held[2][...], preferred_element_type=F32)
    moved_ref[rows:, :] = jnp.zeros((8, hidden), F32)
    dh = moved_ref[shift : shift + rows, :]
    s = jax.nn.sigmoid(g)
    a = g * s
    h = a * u
    sd = dh * p
    pg = jnp.sum(dh * h, axis=1, keepdims=True)
    du_ref[...] = (sd * a).astype(BF16)
    dg_ref[...] = (sd * u * s * (1.0 + g * (1.0 - s))).astype(BF16)
    moved_ref[:8, :] = jnp.zeros((8, hidden), F32)
    moved_ref[shift : shift + rows, :] = h * p
    hp_ref[...] = moved_ref[:rows, :].astype(BF16)
    pg = (pg + jnp.zeros((rows, LANES), F32)).astype(BF16)
    last = iota((8, LANES), 0) == 7
    copies[3].wait()
    copies[4].wait()
    step = next(s for s in (1024, 512, 256, 128) if width % s == 0)
    for start in range(0, width, step):
        cols = slice(start, start + step)
        dx = jnp.dot(dg_ref[...], held[3][:, cols], preferred_element_type=F32)
        dx = dx + jnp.dot(du_ref[...], held[4][:, cols], preferred_element_type=F32)
        for i in range(sources):
            chip = i if joined else info_ref[1 + i] // 2
            part = slice(i * group, (i + 1) * group)
            ret_ref[chip, 0, :, cols] = dx[part, :].astype(BF16)
            if start == 0:
                grads = lax.dot_general(
                    pg[part, :], eye(group), TN, preferred_element_type=F32
                )[:1]
                tail = jnp.where(last, grads, dx[(i + 1) * group - 8 : (i + 1) * group, :LANES])
                ret_ref[chip, 0, group - 8 :, :LANES] = tail.astype(BF16)


def whole(shape):
    return pl.BlockSpec(shape, lambda *_: (0,) * len(shape), pipeline_mode=pl.Buffered(1))


def params(mib):
    return pltpu.CompilerParams(vmem_limit_bytes=mib * 1024 * 1024)


COST = pl.CostEstimate(flops=1024, bytes_accessed=1024, transcendentals=0)


SMEM = pl.BlockSpec(memory_space=pltpu.SMEM)


def call(kernel, info, operands, out_shape, in_specs=None, mib=60):
    return pl.pallas_call(
        kernel,
        grid=(1,),
        in_specs=([SMEM] if info is not None else [])
        + (in_specs or [whole(a.shape) for a in operands]),
        out_specs=[whole(s.shape) for s in out_shape],
        out_shape=out_shape,
        compiler_params=params(mib),
        cost_estimate=COST,
    )(*([info] if info is not None else []), *operands)


def pack(x, dy, ids, probs, nodes, locals_):
    tokens, width = x.shape
    shape = jax.ShapeDtypeStruct((2 * tokens + EXTRA, width), BF16)
    kernel = functools.partial(pack_kernel, nodes, locals_)
    return call(kernel, None, [x, dy, ids, probs], [shape])[0]


def finish(info, ids_t, totals, chips, locals_):
    tokens, width = totals[0].shape[0] - TAIL, totals[0].shape[1]
    shapes = [
        jax.ShapeDtypeStruct((tokens, width), BF16),
        jax.ShapeDtypeStruct(ids_t.shape, BF16),
    ]
    kernel = functools.partial(finish_kernel, chips, locals_)
    grad_x, grad_probs = call(kernel, info, [ids_t, *totals], shapes, mib=24)
    return grad_x, grad_probs.T


def dispatch(at, targets, info, mine, sibling, joined):
    height, width = mine.shape
    if joined:
        shapes = [jax.ShapeDtypeStruct((targets, at.message, width), BF16)]
    else:
        shapes = [jax.ShapeDtypeStruct((at.message, width), BF16)] * targets
    kernel = functools.partial(dispatch_kernel, at, targets)
    out = call(kernel, info, [mine, sibling], shapes)
    return out[0] if joined else out


def combine(at, info, mine, sibling, rets, slot):
    height, width = mine.shape
    tokens = (height - EXTRA) // 2
    shapes = [jax.ShapeDtypeStruct((tokens + TAIL, width), BF16)] * 2
    kernel = functools.partial(combine_kernel, at, rets.shape[0])
    extra = pl.BlockSpec((EXTRA, width), lambda *_: (2 * tokens // EXTRA, 0))
    targets, _, group, _ = rets.shape
    ret = pl.BlockSpec(
        (targets, 1, group, width), lambda *_: (0, slot, 0, 0), pipeline_mode=pl.Buffered(1)
    )
    specs = [extra, extra, ret]
    return call(kernel, info, [mine, sibling, rets], shapes, specs, 24)


def expert(at, info, msgs, weights, saved, chunk, chunks, slot, slots, ret):
    sources = sum(m.size // (at.message * m.shape[-1]) for m in msgs)
    width = msgs[0].shape[-1]
    hidden = weights[0].shape[2]
    rows = sources * at.group
    wide_spec, thin_spec = (
        pl.BlockSpec((rows, n), lambda *_: (chunk, 0), pipeline_mode=pl.Buffered(1))
        for n in (width, hidden)
    )
    out_shape = [jax.ShapeDtypeStruct((sources, slots, at.group, width), BF16)]
    ret_spec = pl.BlockSpec(
        (sources, 1, at.group, width), lambda *_: (0, slot, 0, 0), pipeline_mode=pl.Buffered(1)
    )
    out_specs = [ret_spec] + [wide_spec] * 2 + [thin_spec] * 3
    out_shape += [jax.ShapeDtypeStruct((chunks * rows, width), BF16)] * 2
    out_shape += [jax.ShapeDtypeStruct((chunks * rows, hidden), BF16)] * 3
    in_specs = [SMEM] + [whole(m.shape) for m in msgs]
    first = 1 + len(msgs) + 5
    aliases = {first + i: 1 + i for i in range(len(saved))}
    kept = list(saved)
    if ret is not None:
        aliases[first + len(saved)] = 0
        kept.append(ret)
    in_specs += [pl.BlockSpec(memory_space=pl.ANY)] * (5 + len(kept))
    out = pl.pallas_call(
        functools.partial(expert_kernel, at, sources, len(kept)),
        grid=(1,),
        in_specs=in_specs,
        out_specs=out_specs,
        out_shape=out_shape,
        input_output_aliases=aliases,
        scratch_shapes=[pltpu.VMEM(w.shape, BF16) for w in weights]
        + [pltpu.VMEM((rows + 8, hidden), F32), pltpu.SemaphoreType.DMA((5,))],
        compiler_params=params(60),
        cost_estimate=COST,
    )(info, *msgs, *weights, *kept)
    return out[0], out[1:]


def shards(tokens_x, grad_out, expert_ids, probs, w_gate, w_up, w_down):
    nodes, locals_ = lax.axis_size("node"), lax.axis_size("local")
    experts = nodes * locals_
    tokens, top = expert_ids.shape
    width = tokens_x.shape[1]
    at = Rows(tokens * top // experts + 1)
    node, local = lax.axis_index("node"), lax.axis_index("local")
    both = ("node", "local")
    chips = list(range(0, nodes, 2))
    targets = len(chips)

    def swap(value, dn=0, dz=0):
        pairs = [
            (n * locals_ + z, (n ^ dn) * locals_ + (z ^ dz))
            for n in range(nodes)
            for z in range(locals_)
        ]
        return lax.ppermute(value, both, pairs)

    def along(value, moves):
        pairs = [(n * locals_ + a, n * locals_ + b) for n in range(nodes) for a, b in moves]
        return lax.ppermute(value, both, pairs)

    middle = (local == 1) | (local == 2)
    same_core = [list(range(core, nodes, 2)) for core in range(2)]

    def back(value):
        return lax.all_to_all(
            value, "node", split_axis=0, concat_axis=0, axis_index_groups=same_core, tiled=True
        )

    def fence(*values):
        return lax.optimization_barrier(values)

    ids_t = expert_ids.T
    info = jnp.concatenate([local[None], node ^ jnp.array(chips, jnp.int32)]).astype(jnp.int32)
    payload = pack(tokens_x, grad_out, ids_t, probs.T, nodes, locals_)

    def sisters(block):
        return swap(block, 1)

    def fill(block, sister, joined):
        return dispatch(at, targets, info, block, sister, joined)

    def send(msgs):
        return [msgs[0]] + [swap(msgs[j], chips[j]) for j in range(1, targets)]

    def turn(token):
        down, gate, up, _ = fence(w_down, w_gate, w_up, token)
        return [w_gate, w_up, down[0].T, gate[0].T, up[0].T]

    def work(c, msgs, weights, saved, slot=0, slots=1, ret=None):
        return expert(at, info, msgs, weights, saved, c, locals_, slot, slots, ret)

    def merge(block, sister, ret, slot=0):
        return combine(at, info, block, sister, ret, slot)

    (go,) = fence(node < nodes)

    def at_once(step, *args):
        shapes = jax.eval_shape(step, *args)
        idle = lambda *_: jax.tree.map(lambda v: jnp.zeros(v.shape, v.dtype), shapes)
        return lax.cond(go, step, idle, *args)

    def prepare(block, joined=False):
        def step(block):
            sister = sisters(block)
            return sister, fill(block, sister, joined)

        return at_once(step, block)

    def home(*parts):
        def step(parts):
            moved = [swap(other, 1) for _, other in parts]
            return [
                (keep.astype(F32) + other.astype(F32)).astype(BF16)
                for (keep, _), other in zip(parts, moved)
            ]

        return at_once(step, parts)

    def wgrad(a, b):
        return lax.dot_general(a, b, TN, preferred_element_type=F32).astype(BF16)

    if locals_ == 4:
        b0 = payload
        b1, inner = swap(b0, 0, 1), along(b0, [(1, 2), (2, 1)])
        s0, m0 = prepare(b0, joined=True)
        p0 = back(m0)
        weights = turn(m0)
        b1, inner, weights = fence(b1, inner, weights)
        outward, inner2 = along(inner, [(1, 0), (2, 3)]), along(b1, [(1, 2), (2, 1)])
        s1, m1 = prepare(b1)
        p0, m1 = fence(p0, m1)
        p1 = send(m1)
        r0, saved = work(0, [p0], weights, ())
        outward, inner2, r0 = fence(outward, inner2, r0)
        b2 = jnp.where(middle, inner2, outward)
        b3 = swap(b2, 0, 1)
        s2, m2 = prepare(b2)
        p1, m2, r0, saved = fence(p1, m2, r0, saved)
        p2 = send(m2)
        r1, saved = work(1, p1, weights, saved, 0, 2)
        b3, r1 = fence(b3, r1)
        s3, m3 = prepare(b3)
        p2, m3, r1, saved = fence(p2, m3, r1, saved)
        p3 = send(m3)
        r2, saved = work(2, p2, weights, saved)
        p3, r2, saved = fence(p3, r2, saved)
        r2 = back(r2)
        r13, saved = work(3, p3, weights, saved, 1, 2, r1)
        r2, r13, saved = fence(r2, r13, saved)
        (t2,) = home(merge(b2, s2, r2))
        t2, r13, saved = fence(t2, r13, saved)
        r13 = back(r13)
        t2 = swap(t2, 0, 2)
        x_all, dy_all, hp, du, dg = saved
        gate_wgrad, up_wgrad = wgrad(x_all, dg), wgrad(x_all, du)
        r13, gate_wgrad, up_wgrad = fence(r13, gate_wgrad, up_wgrad)
        t3, t1 = home(merge(b3, s3, r13, 1), merge(b1, s1, r13, 0))
        t3, t1, t2, r0, dy_all, hp = fence(t3, t1, t2, r0, dy_all, hp)
        t3 = swap(t3, 0, 3)
        t1 = swap(t1, 0, 1)
        r0 = back(r0)
        down_wgrad = wgrad(hp, dy_all)
        r0, down_wgrad = fence(r0, down_wgrad)
        (t0,) = home(merge(b0, s0, r0))
        t0, t1, t2, t3 = fence(t0, t1, t2, t3)
        totals = [t0, t1, t2, t3]
    else:
        weights, saved, totals = turn(payload), (), []
        for c in range(locals_):
            block = swap(payload, 0, c) if c else payload
            sister, msgs = prepare(block)
            ret, saved = work(c, send(msgs), weights, saved)
            (total,) = home(merge(block, sister, back(ret)))
            totals.append(swap(total, 0, c) if c else total)
        x_all, dy_all, hp, du, dg = saved
        gate_wgrad, up_wgrad = wgrad(x_all, dg), wgrad(x_all, du)
        down_wgrad = wgrad(hp, dy_all)

    me = (node * locals_ + local)[None].astype(jnp.int32)
    grad_x, grad_probs = finish(me, ids_t, totals, chips, locals_)
    return (grad_x, grad_probs, gate_wgrad[None], up_wgrad[None], down_wgrad[None])


def solution(mesh):
    row, cube = P(("node", "local"), None), P(("node", "local"), None, None)
    return jax.shard_map(
        shards,
        mesh=mesh,
        in_specs=(row, row, row, row, cube, cube, cube),
        out_specs=(row, row, cube, cube, cube),
        check_vma=False,
    )
```
